32 devices in a mesh: groups: 2 (over x), tm: 8 (over z, y), space: 2 (over core).
Axes of the slice: x: 2, y: 2, z: 4, core: 2. Of those that a mesh axis runs over, the one named last changes fastest.
Arguments:
- initial: float32 [128, 4096], P(('groups', 'space')), parts along dimension 0, may hold values from -6 to 6
- guess: float32 [16, 64, 4096], P(('groups', 'tm'), 'space'), parts along dimension 0, may hold values from -6 to 6
- source: float32 [16, 64, 4096], P(('groups', 'tm'), 'space'), parts along dimension 0, may hold values from -12 to 12
- kappa: float32 [64, 4096], P('space'), may hold values from 0.25 to 1
- speed_x: float32 [64, 4096], P('space'), may hold values from -0.4 to 0.4
- speed_y: float32 [64, 4096], P('space'), may hold values from -0.4 to 0.4
Outputs:
- corrected: float32 [16, 64, 4096], P(('groups', 'tm'), 'space'), parts along dimension 0
- new_residual: float32 [16, 64, 4096], P(('groups', 'tm'), 'space'), parts along dimension 0
The draws below stay inside these ranges and needn't reach their ends.
There are 2 independent parts, one for each index of `groups`. The reference program is written for one: setup_inputs(seed, part) draws one part's arguments, and reference() takes and returns one part's arrays. A program takes and returns all parts, laid end to end along the dimension named above; an argument that names none is the same for every part. Nothing has to cross between parts.
All inputs are finite; a program needn't handle non-finite values.
Results may differ from the reference program's by a relative error of at most 0.000031.
Values sent between devices are 32-bit elements; how exact they have to be, the bound alone decides.
A program may use at most 64 MiB of HBM per device.

```python
import math
import jax
import jax.numpy as jnp
from jax import lax

NX = 4096
SUB = 8
NI = 8
NY = 64


def level_of(key, extent, pieces, low, high):
    def one(axis_at, shards_of):
        heights = jax.random.uniform(jax.random.fold_in(jax.random.fold_in(key, 6), axis_at), (shards_of,), jnp.float32, low / len(pieces), high / len(pieces))
        return jnp.repeat(jnp.exp(heights), extent[axis_at] // shards_of).reshape((-1,) + (1,) * (len(extent) - axis_at - 1))

    loudness = one(*pieces[0])
    for cut in pieces[1:]:
        loudness = loudness * one(*cut)
    return loudness


def normal_values(rng, shape, deviation, limit, split=(), dtype=jnp.bfloat16):
    array = jax.random.normal(rng, shape, jnp.float32) * deviation
    if len(split) > 0:
        array = level_of(rng, shape, split, -0.22, 0.18) * array
    return jnp.clip(array, min=-limit, max=limit).astype(dtype)


def setup_inputs(seed: int = 0, part: int = 0) -> dict:
    arg_keys = jax.random.split(jax.random.key(seed), 7)
    part_keys = jax.random.split(jax.random.fold_in(arg_keys[6], part), 7)
    initial = normal_values(part_keys[0], (NY, NX), 1.0, 6.0, ((0, 2),), jnp.float32)
    guess = normal_values(part_keys[1], (NI, NY, NX), 1.0, 6.0, ((0, 8), (1, 2)), jnp.float32)
    source = normal_values(part_keys[2], (NI, NY, NX), 2.0, 12.0, ((0, 8), (1, 2)), jnp.float32)
    kappa = jnp.clip(jnp.exp(math.log(1.0) - 1.3862944 * jax.random.uniform(arg_keys[3], (NY, NX), jnp.float32) ** level_of(arg_keys[3], (NY, NX), ((0, 2),), -0.2, 0.2)), 0.25, 1.0)
    speed_x = jnp.clip(jax.random.uniform(arg_keys[4], (NY, NX), jnp.float32, -0.4, 0.4) * level_of(arg_keys[4], (NY, NX), ((0, 2),), -0.4, 0.0), -0.4, 0.4)
    speed_y = jnp.clip(jax.random.uniform(arg_keys[5], (NY, NX), jnp.float32, -0.4, 0.4) * level_of(arg_keys[5], (NY, NX), ((0, 2),), -0.4, 0.0), -0.4, 0.4)
    return {"initial": initial, "guess": guess, "source": source, "kappa": kappa, "speed_x": speed_x, "speed_y": speed_y}


fine_tau = 0.025


def face_terms(kappa):
    padded = jnp.pad(kappa, 1)
    north = 0.5 * (kappa + padded[:-2, 1:-1])
    south = 0.5 * (kappa + padded[2:, 1:-1])
    west = 0.5 * (kappa + padded[1:-1, :-2])
    east = 0.5 * (kappa + padded[1:-1, 2:])
    return north, south, west, east


def advance(field, faces, speed_x, speed_y, tau, drive_src):
    padded = jnp.pad(field, 1)
    up_row = padded[:-2, 1:-1]
    down_row = padded[2:, 1:-1]
    left_col = padded[1:-1, :-2]
    right_col = padded[1:-1, 2:]
    flux = faces[0] * (up_row - field) + faces[1] * (down_row - field) + faces[2] * (left_col - field) + faces[3] * (right_col - field)
    adv = 0.5 * (speed_x * (right_col - left_col) + speed_y * (down_row - up_row))
    drive = flux - adv
    if drive_src is not None:
        drive = drive + drive_src
    return field + tau * drive


def reference(initial, guess, source, kappa, speed_x, speed_y):
    faces = face_terms(kappa)

    def interval(pair):
        start, src = pair
        return lax.fori_loop(0, SUB, lambda turn, u: advance(u, faces, speed_x, speed_y, fine_tau, src), start)

    starts = jnp.concatenate([initial[None], guess[:-1]], axis=0)
    ends = lax.map(interval, (starts, source))
    resid = ends - guess

    def link(err, res):
        err = advance(err, faces, speed_x, speed_y, SUB * fine_tau, None) + res
        return err, err

    zero = jnp.zeros(initial.shape, jnp.float32)
    unused, err = lax.scan(link, zero, resid)
    corrected = guess + err
    starts_new = jnp.concatenate([initial[None], corrected[:-1]], axis=0)
    ends_new = lax.map(interval, (starts_new, source))
    return corrected, ends_new - corrected
```

```python
import functools
import jax
import jax.numpy as jnp
from jax import lax
from jax.experimental import pallas as pl
from jax.experimental.pallas import tpu as pltpu
from jax.sharding import PartitionSpec as P

SUB = 8
FINE_TAU = 0.025
MESH = pl.DeviceIdType.MESH
HALO = 8
PAD = 256
SWEEP = 512
CHUNK = 256


def kernel(
    count,
    init_ref, guess_ref, src_ref, kap_ref, sx_ref, sy_ref,
    cor_ref, res_ref,
    st, kb, xb, yb, ts, ua, ub, an, as_, aw, ae, c0, dd, rr, ex, ee, rs, er, eh,
    sib_send, sib_recv, g_send, g_recv, gh_send, gh_recv, r_send, r_recv, rh_send, rh_recv,
    x_send, x_recv, xh_send, xh_recv, e_send, e_recv, h_send, h_recv,
):
    j = lax.axis_index("tm")
    s = lax.axis_index("space")
    n = guess_ref.shape[1]
    rows = guess_ref.shape[0]
    tall = rows + HALO
    chunks = n // CHUNK
    odd = lax.rem(j, 2) == 1
    even = lax.rem(j, 2) == 0
    own = pl.multiple_of(HALO * s, HALO)
    hal = pl.multiple_of(rows * (1 - s), HALO)
    bnd = pl.multiple_of((rows - HALO) * (1 - s), HALO)
    edge = pl.multiple_of((rows - HALO) * (1 - s) + HALO * s, HALO)
    there = pl.multiple_of(rows * s, HALO)

    def dev(step):
        return {"tm": lax.rem(j + step + count, count)}

    sibling = {"space": 1 - s}

    barrier = pltpu.get_barrier_semaphore()
    greeted = 1
    pl.semaphore_signal(barrier, inc=1, device_id=sibling, device_id_type=MESH)
    for step in (-2, -1, 1, 2):
        there_is = jnp.logical_and(j + step >= 0, j + step < count)

        @pl.when(there_is)
        def _(step=step):
            pl.semaphore_signal(barrier, inc=1, device_id=dev(step), device_id_type=MESH)

        greeted = greeted + there_is.astype(jnp.int32)
    pl.semaphore_wait(barrier, greeted)

    def remote(src, dst, send, recv, device):
        return pltpu.make_async_remote_copy(
            src_ref=src, dst_ref=dst, send_sem=send, recv_sem=recv,
            device_id=device, device_id_type=MESH,
        )

    def cols(c, pad):
        return pl.ds(pl.multiple_of(pad + c * CHUNK, 128), CHUNK)

    def ownr():
        return pl.ds(own, rows)

    def guess_copy(c):
        return remote(guess_ref.at[:, cols(c, 0)], st.at[ownr(), cols(c, PAD)],
                      g_send.at[c], g_recv.at[c], dev(1))

    def forward(buf, send, recv, c):
        return remote(buf.at[pl.ds(edge, HALO), cols(c, PAD)],
                      buf.at[pl.ds(there, HALO), cols(c, PAD)],
                      send.at[c], recv.at[c], sibling)

    def landed(buf, send, recv, c):
        return remote(buf.at[pl.ds(edge, HALO), cols(c, PAD)],
                      buf.at[pl.ds(hal, HALO), cols(c, PAD)],
                      send.at[c], recv.at[c], sibling)

    def r_copy(c):
        return remote(rs.at[:, cols(c, PAD)], rr.at[ownr(), cols(c, PAD)],
                      r_send.at[c], r_recv.at[c], dev(1))

    def x_copy(c):
        return remote(er.at[:, cols(c, 0)], ex.at[ownr(), cols(c, PAD)],
                      x_send.at[c], x_recv.at[c], dev(2))

    def e_copy(c):
        return remote(ex.at[ownr(), cols(c, PAD)], ee.at[ownr(), cols(c, PAD)],
                      e_send.at[c], e_recv.at[c], dev(-1))

    def h_copy(c):
        return remote(ee.at[pl.ds(edge, HALO), cols(c, PAD)], eh.at[:, cols(c, 0)],
                      h_send.at[c], h_recv.at[c], sibling)

    has_next = j < count - 1

    @pl.when(has_next)
    def _():
        @pl.loop(0, chunks)
        def _(c):
            guess_copy(c).start()

    given = ((kap_ref, kb), (sx_ref, xb), (sy_ref, yb), (src_ref, ts))

    def sib_copy(at, send_side):
        a, b = given[at]
        return remote(a.at[pl.ds(bnd, HALO), :],
                      b.at[pl.ds(there if send_side else hal, HALO), pl.ds(PAD, n)],
                      sib_send.at[at], sib_recv.at[at], sibling)

    for at in range(4):
        sib_copy(at, True).start()
    for buf in (st, kb, ua, ub, an, as_, aw, ae, dd, rr, ex, ee):
        buf[:, :PAD] = jnp.zeros((tall, PAD), jnp.float32)
        buf[:, PAD + n:] = jnp.zeros((tall, PAD), jnp.float32)
    for a, b in given:
        b[ownr(), PAD:PAD + n] = a[...]

    @pl.when(j == 0)
    def _():
        st[ownr(), PAD:PAD + n] = init_ref[...]
        ee[:, PAD:PAD + n] = jnp.zeros((tall, n), jnp.float32)

        @pl.loop(0, chunks)
        def _(c):
            forward(st, gh_send, gh_recv, c).start()

    @pl.when(j == 1)
    def _():
        ex[:, PAD:PAD + n] = jnp.zeros((tall, n), jnp.float32)

    for at in range(4):
        sib_copy(at, False).wait_recv()

    def wide(buf, lo, width):
        return buf[:, pl.ds(pl.multiple_of(lo - 128, 128), width + 256)]

    def sides(block, width):
        left = pltpu.roll(block, 1, 1)[:, 128:128 + width]
        right = pltpu.roll(block, width + 255, 1)[:, 128:128 + width]
        middle = block[:, 128:128 + width]
        return middle, pltpu.roll(middle, 1, 0), pltpu.roll(middle, tall - 1, 0), left, right

    @pl.loop(0, n // SWEEP)
    def _(c):
        lo = pl.multiple_of(PAD + c * SWEEP, 128)
        at = pl.ds(lo, SWEEP)
        k, kn, ks, kw, ke = sides(wide(kb, lo, SWEEP), SWEEP)
        line = lax.broadcasted_iota(jnp.int32, (tall, SWEEP), 0)
        first, last = line == 0, line == tall - 1
        cn = 0.5 * (k + jnp.where(first, 0.0, kn))
        cs = 0.5 * (k + jnp.where(last, 0.0, ks))
        cw = 0.5 * (k + kw)
        ce = 0.5 * (k + ke)
        sx, sy = 0.5 * xb[:, at], 0.5 * yb[:, at]
        an[:, at] = jnp.where(first, 0.0, FINE_TAU * (cn + sy))
        as_[:, at] = jnp.where(last, 0.0, FINE_TAU * (cs - sy))
        aw[:, at] = FINE_TAU * (cw + sx)
        ae[:, at] = FINE_TAU * (ce - sx)
        total = FINE_TAU * ((cn + cs) + (cw + ce))
        dd[:, at] = total
        c0[:, at] = 1.0 - total
        ts[:, at] = FINE_TAU * ts[:, at]

    def sweep(a, b):
        @pl.loop(0, n // SWEEP)
        def _(c):
            lo = pl.multiple_of(PAD + c * SWEEP, 128)
            at = pl.ds(lo, SWEEP)
            u, un, us, uw, ue = sides(wide(a, lo, SWEEP), SWEEP)
            b[:, at] = ((c0[:, at] * u + ts[:, at]) + (an[:, at] * un + as_[:, at] * us)
                        + (aw[:, at] * uw + ae[:, at] * ue))

    def interval(a):
        sweep(a, ub)

        @pl.loop(0, (SUB - 2) // 2)
        def _(_turn):
            sweep(ub, ua)
            sweep(ua, ub)

        sweep(ub, ua)

    def coarse(buf, lo):
        at = pl.ds(lo, CHUNK)
        u, un, us, uw, ue = sides(wide(buf, lo, CHUNK), CHUNK)
        drive = ((an[:, at] * un + as_[:, at] * us) + (aw[:, at] * uw + ae[:, at] * ue)
                 - dd[:, at] * u)
        return u + float(SUB) * drive

    @pl.when(j > 0)
    def _():
        @pl.loop(0, chunks)
        def _(c):
            guess_copy(c).wait_recv()
            forward(st, gh_send, gh_recv, c).start()

    @pl.loop(0, chunks)
    def _(c):
        landed(st, gh_send, gh_recv, c).wait_recv()

    interval(st)

    @pl.loop(0, chunks)
    def _(c):
        at = cols(c, PAD)
        rs[:, at] = ua[ownr(), at] - guess_ref[:, cols(c, 0)]

        @pl.when(even)
        def _():
            r_copy(c).start()

    def finish(c):
        at = cols(c, PAD)
        lo = pl.multiple_of(PAD + c * CHUNK, 128)
        ua[:, at] = coarse(ee, lo)
        err = ua[ownr(), at] + rs[:, at]
        cor_ref[:, cols(c, 0)] = guess_ref[:, cols(c, 0)] + err
        return err

    sends_x = jnp.logical_and(odd, j + 2 < count)
    takes_x = jnp.logical_and(odd, j > 1)
    takes_e = jnp.logical_and(even, j > 0)

    @pl.when(odd)
    def _():
        @pl.loop(0, chunks + 1)
        def _(c):
            @pl.when(c < chunks)
            def _():
                r_copy(c).wait_recv()
                forward(rr, rh_send, rh_recv, c).start()

                @pl.when(takes_x)
                def _():
                    x_copy(c).wait_recv()
                    forward(ex, xh_send, xh_recv, c).start()
                    e_copy(c).start()

                landed(rr, rh_send, rh_recv, c).wait_recv()

                @pl.when(takes_x)
                def _():
                    landed(ex, xh_send, xh_recv, c).wait_recv()

            lo = pl.multiple_of(PAD - 128 + c * CHUNK, 128)
            at = pl.ds(lo, CHUNK)
            ee[:, at] = coarse(ex, lo) + rr[:, at]

            @pl.when(c > 0)
            def _():
                h_copy(c - 1).start()
                er[:, cols(c - 1, 0)] = finish(c - 1)

                @pl.when(sends_x)
                def _():
                    x_copy(c - 1).start()

        @pl.loop(0, chunks)
        def _(c):
            h_copy(c).wait_recv()
            at = cols(c, PAD)
            ua[:, at] = st[:, at] + ee[:, at]
            ua[pl.ds(hal, HALO), at] = st[pl.ds(hal, HALO), at] + eh[:, cols(c, 0)]

    @pl.when(even)
    def _():
        @pl.loop(0, chunks + 1)
        def _(c):
            @pl.when(jnp.logical_and(c < chunks, takes_e))
            def _():
                e_copy(c).wait_recv()
                forward(ee, xh_send, xh_recv, c).start()
                landed(ee, xh_send, xh_recv, c).wait_recv()

            @pl.when(c > 0)
            def _():
                finish(c - 1)

        @pl.loop(0, chunks)
        def _(c):
            at = cols(c, PAD)
            ua[:, at] = st[:, at] + ee[:, at]

    interval(ua)

    @pl.loop(0, chunks)
    def _(c):
        at = cols(c, 0)
        res_ref[:, at] = ua[ownr(), cols(c, PAD)] - cor_ref[:, at]

    for at in range(4):
        sib_copy(at, True).wait_send()

    @pl.loop(0, chunks)
    def _(c):
        forward(st, gh_send, gh_recv, c).wait_send()

        @pl.when(has_next)
        def _():
            guess_copy(c).wait_send()

        @pl.when(even)
        def _():
            r_copy(c).wait_send()

        @pl.when(odd)
        def _():
            forward(rr, rh_send, rh_recv, c).wait_send()
            h_copy(c).wait_send()

        @pl.when(takes_x)
        def _():
            forward(ex, xh_send, xh_recv, c).wait_send()
            e_copy(c).wait_send()

        @pl.when(sends_x)
        def _():
            x_copy(c).wait_send()

        @pl.when(takes_e)
        def _():
            forward(ee, xh_send, xh_recv, c).wait_send()


def local(initial, guess, source, kappa, speed_x, speed_y):
    count = lax.axis_size("tm")
    rows, n = kappa.shape
    chunks = n // CHUNK
    tall = rows + HALO
    big = pltpu.VMEM((tall, n + 2 * PAD), jnp.float32)
    sems = pltpu.SemaphoreType.DMA
    cor, res = pl.pallas_call(
        functools.partial(kernel, count),
        out_shape=[jax.ShapeDtypeStruct((rows, n), jnp.float32)] * 2,
        in_specs=[pl.BlockSpec(memory_space=pltpu.VMEM)] * 6,
        out_specs=[pl.BlockSpec(memory_space=pltpu.VMEM)] * 2,
        scratch_shapes=[big] * 16 + [
            pltpu.VMEM((rows, n + 2 * PAD), jnp.float32),
            pltpu.VMEM((rows, n), jnp.float32),
            pltpu.VMEM((HALO, n), jnp.float32),
        ] + [sems((4,))] * 2 + [sems((chunks,))] * 16,
        compiler_params=pltpu.CompilerParams(
            collective_id=0, has_side_effects=True, vmem_limit_bytes=40 * 1024 * 1024
        ),
    )(initial, guess[0], source[0], kappa, speed_x, speed_y)
    return cor[None], res[None]


def solution(mesh):
    in_specs = (
        P(("groups", "space"), None),
        P(("groups", "tm"), "space", None),
        P(("groups", "tm"), "space", None),
        P("space", None),
        P("space", None),
        P("space", None),
    )
    out_specs = (P(("groups", "tm"), "space", None), P(("groups", "tm"), "space", None))
    return jax.shard_map(local, mesh=mesh, in_specs=in_specs, out_specs=out_specs, check_vma=False)
```

```python
import functools
import jax
import jax.numpy as jnp
from jax import lax
from jax.experimental import pallas as pl
from jax.experimental.pallas import tpu as pltpu
from jax.sharding import PartitionSpec as P

SUB = 8
FINE_TAU = 0.025
MESH = pl.DeviceIdType.MESH
HALO = 8
PAD = 256
SWEEP = 512
CHUNK = 256
GRAIN = 512
WINDOW = 1024


def kernel(
    count,
    init_ref, guess_ref, src_ref, kap_ref, sx_ref, sy_ref,
    cor_ref, res_ref,
    st, kb, xb, yb, ts, an, as_, aw, ae, c0, dd, rr, ex, ee, rs, eh, er, gv, wa, wb, tmp,
    sib_send, sib_recv, load, g_send, g_recv, gh_send, gh_recv, r_send, r_recv, rh_send, rh_recv,
    x_send, x_recv, xh_send, xh_recv, e_send, e_recv, eh_send, eh_recv, h_send, h_recv,
):
    j = lax.axis_index("tm")
    s = lax.axis_index("space")
    rows, n = guess_ref.shape
    tall = rows + HALO
    chunks = n // CHUNK
    grains = n // GRAIN
    windows = n // WINDOW
    per_window = WINDOW // CHUNK
    span = WINDOW + 256
    odd = lax.rem(j, 2) == 1
    even = lax.rem(j, 2) == 0
    own = pl.multiple_of(HALO * s, HALO)
    hal = pl.multiple_of(rows * (1 - s), HALO)
    bnd = pl.multiple_of((rows - HALO) * (1 - s), HALO)
    edge = pl.multiple_of((rows - HALO) * (1 - s) + HALO * s, HALO)
    there = pl.multiple_of(rows * s, HALO)
    ownr = pl.ds(own, rows)
    halr = pl.ds(hal, HALO)
    has_next = j < count - 1
    sends_x = jnp.logical_and(odd, j + 2 < count)
    takes_x = jnp.logical_and(odd, j > 1)
    takes_e = jnp.logical_and(even, j > 0)

    def dev(step):
        return {"tm": lax.rem(j + step + count, count)}

    def across(step):
        return {"tm": lax.rem(j + step + count, count), "space": 1 - s}

    sibling = {"space": 1 - s}
    given = ((kap_ref, kb), (sx_ref, xb), (sy_ref, yb), (src_ref, ts))

    def load_copy(at):
        a, b = given[at]
        return pltpu.make_async_copy(a, b.at[ownr, pl.ds(PAD, n)], load.at[at])

    for at in range(4):
        load_copy(at).start()
    guess_load = pltpu.make_async_copy(guess_ref, gv, load.at[4])
    guess_load.start()
    init_load = pltpu.make_async_copy(init_ref, st.at[ownr, pl.ds(PAD, n)], load.at[5])

    @pl.when(j == 0)
    def _():
        init_load.start()

    barrier = pltpu.get_barrier_semaphore()
    greeted = 1
    pl.semaphore_signal(barrier, inc=1, device_id=sibling, device_id_type=MESH)
    for step in (-2, -1, 1, 2):
        there_is = jnp.logical_and(j + step >= 0, j + step < count)
        twice = step in (-2, 2)

        @pl.when(there_is)
        def _(step=step, twice=twice):
            pl.semaphore_signal(barrier, inc=1, device_id=dev(step), device_id_type=MESH)
            if twice:
                pl.semaphore_signal(barrier, inc=1, device_id=across(step), device_id_type=MESH)

        greeted = greeted + there_is.astype(jnp.int32) * (2 if twice else 1)
    pl.semaphore_wait(barrier, greeted)

    def remote(src, dst, send, recv, device):
        return pltpu.make_async_remote_copy(
            src_ref=src, dst_ref=dst, send_sem=send, recv_sem=recv,
            device_id=device, device_id_type=MESH,
        )

    def cols(c, pad, width=CHUNK):
        return pl.ds(pl.multiple_of(pad + c * width, 128), width)

    def guess_copy(g):
        return remote(guess_ref.at[:, cols(g, 0, GRAIN)], st.at[ownr, cols(g, PAD, GRAIN)],
                      g_send.at[g], g_recv.at[g], dev(1))

    def init_copy(g):
        return remote(init_ref.at[pl.ds(bnd, HALO), cols(g, 0, GRAIN)],
                      st.at[pl.ds(there, HALO), cols(g, PAD, GRAIN)],
                      gh_send.at[g], gh_recv.at[g], sibling)

    def forward(buf, send, recv, c, width=CHUNK):
        return remote(buf.at[pl.ds(edge, HALO), cols(c, PAD, width)],
                      buf.at[pl.ds(there, HALO), cols(c, PAD, width)],
                      send.at[c], recv.at[c], sibling)

    def landed(buf, send, recv, c, width=CHUNK):
        return remote(buf.at[pl.ds(edge, HALO), cols(c, PAD, width)],
                      buf.at[halr, cols(c, PAD, width)],
                      send.at[c], recv.at[c], sibling)

    def r_copy(c):
        return remote(rs.at[:, cols(c, PAD)], rr.at[ownr, cols(c, PAD)],
                      r_send.at[c], r_recv.at[c], dev(1))

    def x_copy(c):
        return remote(er.at[:, cols(c, 0)], ex.at[ownr, cols(c, PAD)],
                      x_send.at[c], x_recv.at[c], dev(2))

    def xh_copy(c, rows_there):
        return remote(er.at[pl.ds(bnd, HALO), cols(c, 0)],
                      ex.at[pl.ds(rows_there, HALO), cols(c, PAD)],
                      xh_send.at[c], xh_recv.at[c], across(2))

    def e_copy(c):
        return remote(ex.at[ownr, cols(c, PAD)], ee.at[ownr, cols(c, PAD)],
                      e_send.at[c], e_recv.at[c], dev(-1))

    def h_copy(c):
        return remote(ee.at[pl.ds(edge, HALO), cols(c, PAD)], eh.at[:, cols(c, PAD)],
                      h_send.at[c], h_recv.at[c], sibling)

    @pl.when(has_next)
    def _():
        @pl.loop(0, grains)
        def _(g):
            guess_copy(g).start()

    def sib_copy(at, send_side):
        a, b = given[at]
        return remote(a.at[pl.ds(bnd, HALO), :],
                      b.at[pl.ds(there if send_side else hal, HALO), pl.ds(PAD, n)],
                      sib_send.at[at], sib_recv.at[at], sibling)

    for at in range(4):
        sib_copy(at, True).start()
    for buf in (st, kb, an, as_, aw, ae, c0, dd, ts, rr, ex, ee):
        buf[:, :PAD] = jnp.zeros((tall, PAD), jnp.float32)
        buf[:, PAD + n:] = jnp.zeros((tall, PAD), jnp.float32)
    eh[:, :PAD] = jnp.zeros((HALO, PAD), jnp.float32)
    eh[:, PAD + n:] = jnp.zeros((HALO, PAD), jnp.float32)

    @pl.when(j == 0)
    def _():
        ee[:, PAD:PAD + n] = jnp.zeros((tall, n), jnp.float32)

        @pl.loop(0, grains)
        def _(g):
            init_copy(g).start()

    @pl.when(j == 1)
    def _():
        ex[:, PAD:PAD + n] = jnp.zeros((tall, n), jnp.float32)

    for at in range(4):
        load_copy(at).wait()
    for at in range(4):
        sib_copy(at, False).wait_recv()

    def sides(block, width):
        left = pltpu.roll(block, 1, 1)[:, 128:128 + width]
        right = pltpu.roll(block, width + 255, 1)[:, 128:128 + width]
        middle = block[:, 128:128 + width]
        return middle, pltpu.roll(middle, 1, 0), pltpu.roll(middle, tall - 1, 0), left, right

    def wide(buf, lo, width):
        return buf[:, pl.ds(pl.multiple_of(lo - 128, 128), width + 256)]

    @pl.loop(0, n // SWEEP)
    def _(c):
        lo = pl.multiple_of(PAD + c * SWEEP, 128)
        at = pl.ds(lo, SWEEP)
        k, kn, ks, kw, ke = sides(wide(kb, lo, SWEEP), SWEEP)
        line = lax.broadcasted_iota(jnp.int32, (tall, SWEEP), 0)
        first, last = line == 0, line == tall - 1
        cn = 0.5 * (k + jnp.where(first, 0.0, kn))
        cs = 0.5 * (k + jnp.where(last, 0.0, ks))
        cw = 0.5 * (k + kw)
        ce = 0.5 * (k + ke)
        sx, sy = 0.5 * xb[:, at], 0.5 * yb[:, at]
        an[:, at] = jnp.where(first, 0.0, FINE_TAU * (cn + sy))
        as_[:, at] = jnp.where(last, 0.0, FINE_TAU * (cs - sy))
        aw[:, at] = FINE_TAU * (cw + sx)
        ae[:, at] = FINE_TAU * (ce - sx)
        total = FINE_TAU * ((cn + cs) + (cw + ce))
        dd[:, at] = total
        c0[:, at] = 1.0 - total
        ts[:, at] = FINE_TAU * ts[:, at]

    def fine(at):
        def step(a, b):
            u = a[...]
            un, us = pltpu.roll(u, 1, 0), pltpu.roll(u, tall - 1, 0)
            uw, ue = pltpu.roll(u, 1, 1), pltpu.roll(u, span - 1, 1)
            b[...] = ((c0[:, at] * u + ts[:, at]) + (an[:, at] * un + as_[:, at] * us)
                      + (aw[:, at] * uw + ae[:, at] * ue))

        @pl.loop(0, SUB // 2)
        def _(_turn):
            step(wa, wb)
            step(wb, wa)

    def window_at(w):
        return pl.ds(pl.multiple_of(PAD - 128 + w * WINDOW, 128), span)

    def coarse(buf, lo):
        at = pl.ds(lo, CHUNK)
        u, un, us, uw, ue = sides(wide(buf, lo, CHUNK), CHUNK)
        drive = ((an[:, at] * un + as_[:, at] * us) + (aw[:, at] * uw + ae[:, at] * ue)
                 - dd[:, at] * u)
        return u + float(SUB) * drive

    guess_load.wait()

    @pl.when(j == 0)
    def _():
        init_load.wait()

    def first_window(w):
        at = window_at(w)
        wa[...] = st[:, at]
        fine(at)
        rs[:, cols(w, PAD, WINDOW)] = (wa[ownr, 128:128 + WINDOW]
                                       - gv[:, cols(w, 0, WINDOW)])

        @pl.when(even)
        def _():
            @pl.loop(0, per_window)
            def _(i):
                r_copy(w * per_window + i).start()

    @pl.loop(0, grains + 1)
    def _(g):
        @pl.when(g < grains)
        def _():
            @pl.when(j > 0)
            def _():
                guess_copy(g).wait_recv()
                forward(st, gh_send, gh_recv, g, GRAIN).start()

            landed(st, gh_send, gh_recv, g, GRAIN).wait_recv()

        ratio = WINDOW // GRAIN

        @pl.when(jnp.logical_and(lax.rem(g, ratio) == 0, g > 0))
        def _():
            first_window(g // ratio - 1)

    def finish(c):
        at = cols(c, PAD)
        lo = pl.multiple_of(PAD + c * CHUNK, 128)
        tmp[...] = coarse(ee, lo)
        err = tmp[ownr, :] + rs[:, at]
        cor_ref[:, cols(c, 0)] = gv[:, cols(c, 0)] + err
        return err

    def second_window(w, fresh):
        at = window_at(w)
        wa[...] = st[:, at] + ee[:, at]
        if fresh:
            low = w * per_window + jnp.where(w == 0, 0, 1)
            high = jnp.minimum((w + 1) * per_window + 1, chunks)

            @pl.loop(low, high)
            def _(c):
                h_copy(c).wait_recv()

            wa[halr, :] = st[halr, at] + eh[:, at]
        fine(at)
        out = cols(w, 0, WINDOW)
        res_ref[:, out] = wa[ownr, 128:128 + WINDOW] - cor_ref[:, out]

    @pl.when(odd)
    def _():
        @pl.loop(0, chunks + 1)
        def _(c):
            @pl.when(c < chunks)
            def _():
                r_copy(c).wait_recv()
                forward(rr, rh_send, rh_recv, c).start()

                @pl.when(takes_x)
                def _():
                    x_copy(c).wait_recv()
                    e_copy(c).start()
                    xh_copy(c, hal).wait_recv()

                landed(rr, rh_send, rh_recv, c).wait_recv()

            lo = pl.multiple_of(PAD - 128 + c * CHUNK, 128)
            at = pl.ds(lo, CHUNK)
            ee[:, at] = coarse(ex, lo) + rr[:, at]

            @pl.when(c > 0)
            def _():
                er[:, cols(c - 1, 0)] = finish(c - 1)

                @pl.when(sends_x)
                def _():
                    x_copy(c - 1).start()
                    xh_copy(c - 1, there).start()

                h_copy(c - 1).start()

            late = per_window + 2
            ready = jnp.logical_and(c >= late, lax.rem(c + 2 * per_window - late, per_window) == 0)

            @pl.when(jnp.logical_and(ready, jnp.logical_not(sends_x)))
            def _():
                second_window((c - late) // per_window, True)

        @pl.loop(jnp.where(sends_x, 0, windows - 1), windows)
        def _(w):
            second_window(w, True)

    @pl.when(even)
    def _():
        @pl.loop(0, chunks + 1)
        def _(c):
            @pl.when(jnp.logical_and(c < chunks, takes_e))
            def _():
                e_copy(c).wait_recv()
                forward(ee, eh_send, eh_recv, c).start()
                landed(ee, eh_send, eh_recv, c).wait_recv()

            @pl.when(c > 0)
            def _():
                finish(c - 1)

            @pl.when(jnp.logical_and(c > 0, lax.rem(c, per_window) == 0))
            def _():
                second_window(c // per_window - 1, False)

    for at in range(4):
        sib_copy(at, True).wait_send()

    @pl.loop(0, grains)
    def _(g):
        forward(st, gh_send, gh_recv, g, GRAIN).wait_send()

        @pl.when(has_next)
        def _():
            guess_copy(g).wait_send()

    @pl.loop(0, chunks)
    def _(c):
        @pl.when(even)
        def _():
            r_copy(c).wait_send()

        @pl.when(odd)
        def _():
            forward(rr, rh_send, rh_recv, c).wait_send()
            h_copy(c).wait_send()

        @pl.when(takes_x)
        def _():
            e_copy(c).wait_send()

        @pl.when(sends_x)
        def _():
            x_copy(c).wait_send()
            xh_copy(c, there).wait_send()

        @pl.when(takes_e)
        def _():
            forward(ee, eh_send, eh_recv, c).wait_send()


def local(initial, guess, source, kappa, speed_x, speed_y):
    count = lax.axis_size("tm")
    rows, n = kappa.shape
    chunks = n // CHUNK
    tall = rows + HALO
    wide_n = n + 2 * PAD
    sems = pltpu.SemaphoreType.DMA

    def vmem(*shape):
        return pltpu.VMEM(shape, jnp.float32)

    cor, res = pl.pallas_call(
        functools.partial(kernel, count),
        out_shape=[jax.ShapeDtypeStruct((rows, n), jnp.float32)] * 2,
        in_specs=[pl.BlockSpec(memory_space=pltpu.HBM)] * 6,
        out_specs=[pl.BlockSpec(memory_space=pltpu.VMEM)] * 2,
        scratch_shapes=[vmem(tall, wide_n)] * 14 + [
            vmem(rows, wide_n), vmem(HALO, wide_n), vmem(rows, n), vmem(rows, n),
            vmem(tall, WINDOW + 256), vmem(tall, WINDOW + 256), vmem(tall, CHUNK),
        ] + [sems((4,))] * 2 + [sems((6,))] + [sems((n // GRAIN,))] * 4 + [sems((chunks,))] * 14,
        compiler_params=pltpu.CompilerParams(
            collective_id=0, has_side_effects=True, vmem_limit_bytes=62 * 1024 * 1024
        ),
    )(initial, guess[0], source[0], kappa, speed_x, speed_y)
    return cor[None], res[None]


def solution(mesh):
    in_specs = (
        P(("groups", "space"), None),
        P(("groups", "tm"), "space", None),
        P(("groups", "tm"), "space", None),
        P("space", None),
        P("space", None),
        P("space", None),
    )
    out_specs = (P(("groups", "tm"), "space", None), P(("groups", "tm"), "space", None))
    return jax.shard_map(local, mesh=mesh, in_specs=in_specs, out_specs=out_specs, check_vma=False)
```

```python
import functools
import jax
import jax.numpy as jnp
from jax import lax
from jax.experimental import pallas as pl
from jax.experimental.pallas import tpu as pltpu
from jax.sharding import PartitionSpec as P

SUB = 8
FINE_TAU = 0.025
MESH = pl.DeviceIdType.MESH
HALO = 8
PAD = 256
SWEEP = 512
CHUNK = 256
GRAIN = 512
WINDOW = 1024


def kernel(
    count,
    init_ref, guess_ref, src_ref, kap_ref, sx_ref, sy_ref,
    cor_ref, res_ref,
    st, kb, xb, yb, ts, an, as_, aw, ae, c0, dd, rr, ex, ee, rs, eh, er, gv, wa, wb, tmp,
    sib_send, sib_recv, load, g_send, g_recv, gh_send, gh_recv, r_send, r_recv, rh_send, rh_recv,
    x_send, x_recv, xh_send, xh_recv, e_send, e_recv, eh_send, eh_recv, h_send, h_recv,
):
    j = lax.axis_index("tm")
    s = lax.axis_index("space")
    rows, n = guess_ref.shape
    tall = rows + HALO
    chunks = n // CHUNK
    grains = n // GRAIN
    windows = n // WINDOW
    per_window = WINDOW // CHUNK
    span = WINDOW + 256
    odd = lax.rem(j, 2) == 1
    even = lax.rem(j, 2) == 0
    own = pl.multiple_of(HALO * s, HALO)
    hal = pl.multiple_of(rows * (1 - s), HALO)
    bnd = pl.multiple_of((rows - HALO) * (1 - s), HALO)
    edge = pl.multiple_of((rows - HALO) * (1 - s) + HALO * s, HALO)
    there = pl.multiple_of(rows * s, HALO)
    ownr = pl.ds(own, rows)
    halr = pl.ds(hal, HALO)
    has_next = j < count - 1
    sends_x = jnp.logical_and(odd, j + 2 < count)
    takes_x = jnp.logical_and(odd, j > 1)
    takes_e = jnp.logical_and(even, j > 0)

    def dev(step):
        return {"tm": lax.rem(j + step + count, count)}

    def across(step):
        return {"tm": lax.rem(j + step + count, count), "space": 1 - s}

    sibling = {"space": 1 - s}
    given = ((kap_ref, kb), (sx_ref, xb), (sy_ref, yb), (src_ref, ts))

    def load_copy(at):
        a, b = given[at]
        return pltpu.make_async_copy(a, b.at[ownr, pl.ds(PAD, n)], load.at[at])

    for at in range(4):
        load_copy(at).start()
    guess_load = pltpu.make_async_copy(guess_ref, gv, load.at[4])
    guess_load.start()
    init_load = pltpu.make_async_copy(init_ref, st.at[ownr, pl.ds(PAD, n)], load.at[5])

    @pl.when(j == 0)
    def _():
        init_load.start()

    barrier = pltpu.get_barrier_semaphore()
    greeted = 1
    pl.semaphore_signal(barrier, inc=1, device_id=sibling, device_id_type=MESH)
    for step in (-2, -1, 1, 2):
        there_is = jnp.logical_and(j + step >= 0, j + step < count)
        twice = step in (-2, 2)

        @pl.when(there_is)
        def _(step=step, twice=twice):
            pl.semaphore_signal(barrier, inc=1, device_id=dev(step), device_id_type=MESH)
            if twice:
                pl.semaphore_signal(barrier, inc=1, device_id=across(step), device_id_type=MESH)

        greeted = greeted + there_is.astype(jnp.int32) * (2 if twice else 1)
    pl.semaphore_wait(barrier, greeted)

    def remote(src, dst, send, recv, device):
        return pltpu.make_async_remote_copy(
            src_ref=src, dst_ref=dst, send_sem=send, recv_sem=recv,
            device_id=device, device_id_type=MESH,
        )

    def cols(c, pad, width=CHUNK):
        return pl.ds(pl.multiple_of(pad + c * width, 128), width)

    def guess_copy(g):
        return remote(guess_ref.at[:, cols(g, 0, GRAIN)], st.at[ownr, cols(g, PAD, GRAIN)],
                      g_send.at[g], g_recv.at[g], dev(1))

    def init_copy(g):
        return remote(init_ref.at[pl.ds(bnd, HALO), cols(g, 0, GRAIN)],
                      st.at[pl.ds(there, HALO), cols(g, PAD, GRAIN)],
                      gh_send.at[g], gh_recv.at[g], sibling)

    def forward(buf, send, recv, c, width=CHUNK):
        return remote(buf.at[pl.ds(edge, HALO), cols(c, PAD, width)],
                      buf.at[pl.ds(there, HALO), cols(c, PAD, width)],
                      send.at[c], recv.at[c], sibling)

    def landed(buf, send, recv, c, width=CHUNK):
        return remote(buf.at[pl.ds(edge, HALO), cols(c, PAD, width)],
                      buf.at[halr, cols(c, PAD, width)],
                      send.at[c], recv.at[c], sibling)

    def r_copy(c):
        return remote(rs.at[:, cols(c, PAD)], rr.at[ownr, cols(c, PAD)],
                      r_send.at[c], r_recv.at[c], dev(1))

    def x_copy(c):
        return remote(er.at[:, cols(c, 0)], ex.at[ownr, cols(c, PAD)],
                      x_send.at[c], x_recv.at[c], dev(2))

    def xh_copy(c, rows_there):
        return remote(er.at[pl.ds(bnd, HALO), cols(c, 0)],
                      ex.at[pl.ds(rows_there, HALO), cols(c, PAD)],
                      xh_send.at[c], xh_recv.at[c], across(2))

    def e_copy(c):
        return remote(ex.at[ownr, cols(c, PAD)], ee.at[ownr, cols(c, PAD)],
                      e_send.at[c], e_recv.at[c], dev(-1))

    def h_copy(c):
        return remote(ee.at[pl.ds(edge, HALO), cols(c, PAD)], eh.at[:, cols(c, PAD)],
                      h_send.at[c], h_recv.at[c], sibling)

    @pl.when(has_next)
    def _():
        @pl.loop(0, grains)
        def _(g):
            guess_copy(g).start()

    def sib_copy(at, send_side):
        a, b = given[at]
        return remote(a.at[pl.ds(bnd, HALO), :],
                      b.at[pl.ds(there if send_side else hal, HALO), pl.ds(PAD, n)],
                      sib_send.at[at], sib_recv.at[at], sibling)

    for at in range(4):
        sib_copy(at, True).start()
    for buf in (st, kb, an, as_, aw, ae, c0, dd, ts, rr, ex, ee):
        buf[:, :PAD] = jnp.zeros((tall, PAD), jnp.float32)
        buf[:, PAD + n:] = jnp.zeros((tall, PAD), jnp.float32)
    for buf in (wa, wb):
        buf[:8, :] = jnp.zeros((8, span), jnp.float32)
        buf[8 + tall:, :] = jnp.zeros((8, span), jnp.float32)
    eh[:, :PAD] = jnp.zeros((HALO, PAD), jnp.float32)
    eh[:, PAD + n:] = jnp.zeros((HALO, PAD), jnp.float32)

    @pl.when(j == 0)
    def _():
        ee[:, PAD:PAD + n] = jnp.zeros((tall, n), jnp.float32)

        @pl.loop(0, grains)
        def _(g):
            init_copy(g).start()

    @pl.when(j == 1)
    def _():
        ex[:, PAD:PAD + n] = jnp.zeros((tall, n), jnp.float32)

    for at in range(4):
        load_copy(at).wait()
    for at in range(4):
        sib_copy(at, False).wait_recv()

    def sides(block, width):
        left = pltpu.roll(block, 1, 1)[:, 128:128 + width]
        right = pltpu.roll(block, width + 255, 1)[:, 128:128 + width]
        middle = block[:, 128:128 + width]
        return middle, pltpu.roll(middle, 1, 0), pltpu.roll(middle, tall - 1, 0), left, right

    def wide(buf, lo, width):
        return buf[:, pl.ds(pl.multiple_of(lo - 128, 128), width + 256)]

    @pl.loop(0, n // SWEEP)
    def _(c):
        lo = pl.multiple_of(PAD + c * SWEEP, 128)
        at = pl.ds(lo, SWEEP)
        k, kn, ks, kw, ke = sides(wide(kb, lo, SWEEP), SWEEP)
        line = lax.broadcasted_iota(jnp.int32, (tall, SWEEP), 0)
        first, last = line == 0, line == tall - 1
        cn = 0.5 * (k + jnp.where(first, 0.0, kn))
        cs = 0.5 * (k + jnp.where(last, 0.0, ks))
        cw = 0.5 * (k + kw)
        ce = 0.5 * (k + ke)
        sx, sy = 0.5 * xb[:, at], 0.5 * yb[:, at]
        an[:, at] = jnp.where(first, 0.0, FINE_TAU * (cn + sy))
        as_[:, at] = jnp.where(last, 0.0, FINE_TAU * (cs - sy))
        aw[:, at] = FINE_TAU * (cw + sx)
        ae[:, at] = FINE_TAU * (ce - sx)
        total = FINE_TAU * ((cn + cs) + (cw + ce))
        dd[:, at] = total
        c0[:, at] = 1.0 - total
        ts[:, at] = FINE_TAU * ts[:, at]

    def fine(at):
        def step(a, b):
            for low in range(0, tall, 8):
                r = slice(low, low + 8)
                u = a[low + 8:low + 16, :]
                un, us = a[low + 7:low + 15, :], a[low + 9:low + 17, :]
                uw, ue = pltpu.roll(u, 1, 1), pltpu.roll(u, span - 1, 1)
                b[low + 8:low + 16, :] = (
                    (c0[r, at] * u + ts[r, at]) + (an[r, at] * un + as_[r, at] * us)
                    + (aw[r, at] * uw + ae[r, at] * ue))

        @pl.loop(0, SUB // 2)
        def _(_turn):
            step(wa, wb)
            step(wb, wa)

    def window_at(w):
        return pl.ds(pl.multiple_of(PAD - 128 + w * WINDOW, 128), span)

    def coarse(buf, lo):
        at = pl.ds(lo, CHUNK)
        u, un, us, uw, ue = sides(wide(buf, lo, CHUNK), CHUNK)
        drive = ((an[:, at] * un + as_[:, at] * us) + (aw[:, at] * uw + ae[:, at] * ue)
                 - dd[:, at] * u)
        return u + float(SUB) * drive

    guess_load.wait()

    @pl.when(j == 0)
    def _():
        init_load.wait()

    def first_window(w):
        at = window_at(w)
        wa[8:8 + tall, :] = st[:, at]
        fine(at)
        rs[:, cols(w, PAD, WINDOW)] = (wa[pl.ds(own + 8, rows), 128:128 + WINDOW]
                                       - gv[:, cols(w, 0, WINDOW)])

        @pl.when(even)
        def _():
            @pl.loop(0, per_window)
            def _(i):
                r_copy(w * per_window + i).start()

    @pl.loop(0, grains + 2)
    def _(i):
        @pl.when(jnp.logical_and(i < grains, j > 0))
        def _():
            guess_copy(i).wait_recv()
            forward(st, gh_send, gh_recv, i, GRAIN).start()

        g = i - 1

        @pl.when(jnp.logical_and(g >= 0, g < grains))
        def _():
            landed(st, gh_send, gh_recv, g, GRAIN).wait_recv()

        ratio = WINDOW // GRAIN

        @pl.when(jnp.logical_and(lax.rem(g + ratio, ratio) == 0, g > 0))
        def _():
            first_window(g // ratio - 1)

    def finish(c):
        at = cols(c, PAD)
        lo = pl.multiple_of(PAD + c * CHUNK, 128)
        tmp[...] = coarse(ee, lo)
        err = tmp[ownr, :] + rs[:, at]
        cor_ref[:, cols(c, 0)] = gv[:, cols(c, 0)] + err
        return err

    def second_window(w, fresh):
        at = window_at(w)
        wa[8:8 + tall, :] = st[:, at] + ee[:, at]
        if fresh:
            low = w * per_window + jnp.where(w == 0, 0, 1)
            high = jnp.minimum((w + 1) * per_window + 1, chunks)

            @pl.loop(low, high)
            def _(c):
                h_copy(c).wait_recv()

            wa[pl.ds(hal + 8, HALO), :] = st[halr, at] + eh[:, at]
        fine(at)
        out = cols(w, 0, WINDOW)
        res_ref[:, out] = wa[pl.ds(own + 8, rows), 128:128 + WINDOW] - cor_ref[:, out]

    @pl.when(odd)
    def _():
        @pl.loop(0, chunks + 2)
        def _(i):
            @pl.when(i < chunks)
            def _():
                r_copy(i).wait_recv()
                forward(rr, rh_send, rh_recv, i).start()

            c = i - 1

            @pl.when(jnp.logical_and(c >= 0, c < chunks))
            def _():
                @pl.when(takes_x)
                def _():
                    x_copy(c).wait_recv()
                    e_copy(c).start()
                    xh_copy(c, hal).wait_recv()

                landed(rr, rh_send, rh_recv, c).wait_recv()

            @pl.when(c >= 0)
            def _():
                lo = pl.multiple_of(PAD - 128 + c * CHUNK, 128)
                at = pl.ds(lo, CHUNK)
                ee[:, at] = coarse(ex, lo) + rr[:, at]

            @pl.when(c > 0)
            def _():
                er[:, cols(c - 1, 0)] = finish(c - 1)

                @pl.when(sends_x)
                def _():
                    x_copy(c - 1).start()
                    xh_copy(c - 1, there).start()

                h_copy(c - 1).start()

            late = per_window + 2
            ready = jnp.logical_and(c >= late, lax.rem(c + 2 * per_window - late, per_window) == 0)

            @pl.when(jnp.logical_and(ready, jnp.logical_not(sends_x)))
            def _():
                second_window((c - late) // per_window, True)

        @pl.loop(jnp.where(sends_x, 0, windows - 1), windows)
        def _(w):
            second_window(w, True)

    @pl.when(even)
    def _():
        @pl.loop(0, chunks + 2)
        def _(i):
            @pl.when(jnp.logical_and(i < chunks, takes_e))
            def _():
                e_copy(i).wait_recv()
                forward(ee, eh_send, eh_recv, i).start()

            c = i - 1

            @pl.when(jnp.logical_and(jnp.logical_and(c >= 0, c < chunks), takes_e))
            def _():
                landed(ee, eh_send, eh_recv, c).wait_recv()

            @pl.when(c > 0)
            def _():
                finish(c - 1)

            @pl.when(jnp.logical_and(c > 0, lax.rem(c + per_window, per_window) == 0))
            def _():
                second_window(c // per_window - 1, False)

    for at in range(4):
        sib_copy(at, True).wait_send()

    @pl.loop(0, grains)
    def _(g):
        forward(st, gh_send, gh_recv, g, GRAIN).wait_send()

        @pl.when(has_next)
        def _():
            guess_copy(g).wait_send()

    @pl.loop(0, chunks)
    def _(c):
        @pl.when(even)
        def _():
            r_copy(c).wait_send()

        @pl.when(odd)
        def _():
            forward(rr, rh_send, rh_recv, c).wait_send()
            h_copy(c).wait_send()

        @pl.when(takes_x)
        def _():
            e_copy(c).wait_send()

        @pl.when(sends_x)
        def _():
            x_copy(c).wait_send()
            xh_copy(c, there).wait_send()

        @pl.when(takes_e)
        def _():
            forward(ee, eh_send, eh_recv, c).wait_send()


def local(initial, guess, source, kappa, speed_x, speed_y):
    count = lax.axis_size("tm")
    rows, n = kappa.shape
    chunks = n // CHUNK
    tall = rows + HALO
    wide_n = n + 2 * PAD
    sems = pltpu.SemaphoreType.DMA

    def vmem(*shape):
        return pltpu.VMEM(shape, jnp.float32)

    cor, res = pl.pallas_call(
        functools.partial(kernel, count),
        out_shape=[jax.ShapeDtypeStruct((rows, n), jnp.float32)] * 2,
        in_specs=[pl.BlockSpec(memory_space=pltpu.HBM)] * 6,
        out_specs=[pl.BlockSpec(memory_space=pltpu.VMEM)] * 2,
        scratch_shapes=[vmem(tall, wide_n)] * 14 + [
            vmem(rows, wide_n), vmem(HALO, wide_n), vmem(rows, n), vmem(rows, n),
            vmem(tall + 16, WINDOW + 256), vmem(tall + 16, WINDOW + 256), vmem(tall, CHUNK),
        ] + [sems((4,))] * 2 + [sems((6,))] + [sems((n // GRAIN,))] * 4 + [sems((chunks,))] * 14,
        compiler_params=pltpu.CompilerParams(
            collective_id=0, has_side_effects=True, vmem_limit_bytes=62 * 1024 * 1024
        ),
    )(initial, guess[0], source[0], kappa, speed_x, speed_y)
    return cor[None], res[None]


def solution(mesh):
    in_specs = (
        P(("groups", "space"), None),
        P(("groups", "tm"), "space", None),
        P(("groups", "tm"), "space", None),
        P("space", None),
        P("space", None),
        P("space", None),
    )
    out_specs = (P(("groups", "tm"), "space", None), P(("groups", "tm"), "space", None))
    return jax.shard_map(local, mesh=mesh, in_specs=in_specs, out_specs=out_specs, check_vma=False)
```

```python
import functools
import jax
import jax.numpy as jnp
from jax import lax
from jax.experimental import pallas as pl
from jax.experimental.pallas import tpu as pltpu
from jax.sharding import PartitionSpec as P

SUB = 8
FINE_TAU = 0.025
MESH = pl.DeviceIdType.MESH
HALO = 8
PAD = 256
SWEEP = 512
CHUNK = 256
GRAIN = 512
WINDOW = 1024


def kernel(
    count,
    init_ref, guess_ref, src_ref, kap_ref, sx_ref, sy_ref,
    cor_ref, res_ref,
    st, kb, xb, yb, ts, an, as_, aw, ae, c0, dd, rr, ex, ee, rs, eh, er, gv, wa, wb, tmp,
    sib_send, sib_recv, load, g_send, g_recv, gh_send, gh_recv, r_send, r_recv, rh_send, rh_recv,
    x_send, x_recv, xh_send, xh_recv, e_send, e_recv, eh_send, eh_recv, h_send, h_recv,
):
    j = lax.axis_index("tm")
    s = lax.axis_index("space")
    rows, n = guess_ref.shape
    tall = rows + HALO
    chunks = n // CHUNK
    grains = n // GRAIN
    windows = n // WINDOW
    per_window = WINDOW // CHUNK
    span = WINDOW + 256
    odd = lax.rem(j, 2) == 1
    even = lax.rem(j, 2) == 0
    own = pl.multiple_of(HALO * s, HALO)
    hal = pl.multiple_of(rows * (1 - s), HALO)
    bnd = pl.multiple_of((rows - HALO) * (1 - s), HALO)
    edge = pl.multiple_of((rows - HALO) * (1 - s) + HALO * s, HALO)
    there = pl.multiple_of(rows * s, HALO)
    ownr = pl.ds(own, rows)
    halr = pl.ds(hal, HALO)
    has_next = j < count - 1
    sends_x = jnp.logical_and(odd, j + 2 < count)
    takes_x = jnp.logical_and(odd, j > 1)
    takes_e = jnp.logical_and(even, j > 0)

    def dev(step):
        return {"tm": lax.rem(j + step + count, count)}

    def across(step):
        return {"tm": lax.rem(j + step + count, count), "space": 1 - s}

    sibling = {"space": 1 - s}
    given = ((kap_ref, kb), (sx_ref, xb), (sy_ref, yb), (src_ref, ts))

    def load_copy(at):
        a, b = given[at]
        return pltpu.make_async_copy(a, b.at[ownr, pl.ds(PAD, n)], load.at[at])

    for at in range(4):
        load_copy(at).start()
    guess_load = pltpu.make_async_copy(guess_ref, gv, load.at[4])
    guess_load.start()
    init_load = pltpu.make_async_copy(init_ref, st.at[ownr, pl.ds(PAD, n)], load.at[5])

    @pl.when(j == 0)
    def _():
        init_load.start()

    barrier = pltpu.get_barrier_semaphore()
    greeted = 1
    pl.semaphore_signal(barrier, inc=1, device_id=sibling, device_id_type=MESH)
    for step in (-2, -1, 1, 2):
        there_is = jnp.logical_and(j + step >= 0, j + step < count)
        twice = step in (-2, 2)

        @pl.when(there_is)
        def _(step=step, twice=twice):
            pl.semaphore_signal(barrier, inc=1, device_id=dev(step), device_id_type=MESH)
            if twice:
                pl.semaphore_signal(barrier, inc=1, device_id=across(step), device_id_type=MESH)

        greeted = greeted + there_is.astype(jnp.int32) * (2 if twice else 1)
    pl.semaphore_wait(barrier, greeted)

    def remote(src, dst, send, recv, device):
        return pltpu.make_async_remote_copy(
            src_ref=src, dst_ref=dst, send_sem=send, recv_sem=recv,
            device_id=device, device_id_type=MESH,
        )

    def cols(c, pad, width=CHUNK):
        return pl.ds(pl.multiple_of(pad + c * width, 128), width)

    def guess_copy(g):
        return remote(guess_ref.at[:, cols(g, 0, GRAIN)], st.at[ownr, cols(g, PAD, GRAIN)],
                      g_send.at[g], g_recv.at[g], dev(1))

    def init_copy(g):
        return remote(init_ref.at[pl.ds(bnd, HALO), cols(g, 0, GRAIN)],
                      st.at[pl.ds(there, HALO), cols(g, PAD, GRAIN)],
                      gh_send.at[g], gh_recv.at[g], sibling)

    def forward(buf, send, recv, c, width=CHUNK):
        return remote(buf.at[pl.ds(edge, HALO), cols(c, PAD, width)],
                      buf.at[pl.ds(there, HALO), cols(c, PAD, width)],
                      send.at[c], recv.at[c], sibling)

    def landed(buf, send, recv, c, width=CHUNK):
        return remote(buf.at[pl.ds(edge, HALO), cols(c, PAD, width)],
                      buf.at[halr, cols(c, PAD, width)],
                      send.at[c], recv.at[c], sibling)

    def r_copy(c):
        return remote(rs.at[:, cols(c, PAD)], rr.at[ownr, cols(c, PAD)],
                      r_send.at[c], r_recv.at[c], dev(1))

    def x_copy(c):
        return remote(er.at[:, cols(c, 0)], ex.at[ownr, cols(c, PAD)],
                      x_send.at[c], x_recv.at[c], dev(2))

    def xh_copy(c, rows_there):
        return remote(er.at[pl.ds(bnd, HALO), cols(c, 0)],
                      ex.at[pl.ds(rows_there, HALO), cols(c, PAD)],
                      xh_send.at[c], xh_recv.at[c], across(2))

    def e_copy(c):
        return remote(ex.at[ownr, cols(c, PAD)], ee.at[ownr, cols(c, PAD)],
                      e_send.at[c], e_recv.at[c], dev(-1))

    def h_copy(c):
        return remote(ee.at[pl.ds(edge, HALO), cols(c, PAD)], eh.at[:, cols(c, PAD)],
                      h_send.at[c], h_recv.at[c], sibling)

    @pl.when(has_next)
    def _():
        @pl.loop(0, grains)
        def _(g):
            guess_copy(g).start()

    def sib_copy(at, send_side):
        a, b = given[at]
        return remote(a.at[pl.ds(bnd, HALO), :],
                      b.at[pl.ds(there if send_side else hal, HALO), pl.ds(PAD, n)],
                      sib_send.at[at], sib_recv.at[at], sibling)

    for at in range(4):
        sib_copy(at, True).start()
    for buf in (st, kb, an, as_, aw, ae, c0, dd, ts, rr, ex, ee):
        buf[:, :PAD] = jnp.zeros((tall, PAD), jnp.float32)
        buf[:, PAD + n:] = jnp.zeros((tall, PAD), jnp.float32)
    for buf in (wa, wb):
        buf[:8, :] = jnp.zeros((8, span), jnp.float32)
        buf[8 + tall:, :] = jnp.zeros((8, span), jnp.float32)
    eh[:, :PAD] = jnp.zeros((HALO, PAD), jnp.float32)
    eh[:, PAD + n:] = jnp.zeros((HALO, PAD), jnp.float32)

    @pl.when(j == 0)
    def _():
        ee[:, PAD:PAD + n] = jnp.zeros((tall, n), jnp.float32)

        @pl.loop(0, grains)
        def _(g):
            init_copy(g).start()

    @pl.when(j == 1)
    def _():
        ex[:, PAD:PAD + n] = jnp.zeros((tall, n), jnp.float32)

    for at in range(4):
        load_copy(at).wait()
    for at in range(4):
        sib_copy(at, False).wait_recv()

    def sides(block, width):
        left = pltpu.roll(block, 1, 1)[:, 128:128 + width]
        right = pltpu.roll(block, width + 255, 1)[:, 128:128 + width]
        middle = block[:, 128:128 + width]
        return middle, pltpu.roll(middle, 1, 0), pltpu.roll(middle, tall - 1, 0), left, right

    def wide(buf, lo, width):
        return buf[:, pl.ds(pl.multiple_of(lo - 128, 128), width + 256)]

    @pl.loop(0, n // SWEEP)
    def _(c):
        lo = pl.multiple_of(PAD + c * SWEEP, 128)
        at = pl.ds(lo, SWEEP)
        k, kn, ks, kw, ke = sides(wide(kb, lo, SWEEP), SWEEP)
        line = lax.broadcasted_iota(jnp.int32, (tall, SWEEP), 0)
        first, last = line == 0, line == tall - 1
        cn = 0.5 * (k + jnp.where(first, 0.0, kn))
        cs = 0.5 * (k + jnp.where(last, 0.0, ks))
        cw = 0.5 * (k + kw)
        ce = 0.5 * (k + ke)
        sx, sy = 0.5 * xb[:, at], 0.5 * yb[:, at]
        an[:, at] = jnp.where(first, 0.0, FINE_TAU * (cn + sy))
        as_[:, at] = jnp.where(last, 0.0, FINE_TAU * (cs - sy))
        aw[:, at] = FINE_TAU * (cw + sx)
        ae[:, at] = FINE_TAU * (ce - sx)
        total = FINE_TAU * ((cn + cs) + (cw + ce))
        dd[:, at] = total
        c0[:, at] = 1.0 - total
        ts[:, at] = FINE_TAU * ts[:, at]

    def fine(at):
        def step(a, b):
            for low in range(0, tall, 8):
                r = slice(low, low + 8)
                u = a[low + 8:low + 16, :]
                un, us = a[low + 7:low + 15, :], a[low + 9:low + 17, :]
                uw, ue = pltpu.roll(u, 1, 1), pltpu.roll(u, span - 1, 1)
                b[low + 8:low + 16, :] = (
                    (c0[r, at] * u + ts[r, at]) + (an[r, at] * un + as_[r, at] * us)
                    + (aw[r, at] * uw + ae[r, at] * ue))

        @pl.loop(0, SUB // 2)
        def _(_turn):
            step(wa, wb)
            step(wb, wa)

    def window_at(w):
        return pl.ds(pl.multiple_of(PAD - 128 + w * WINDOW, 128), span)

    def coarse(buf, lo):
        at = pl.ds(lo, CHUNK)
        u, un, us, uw, ue = sides(wide(buf, lo, CHUNK), CHUNK)
        drive = ((an[:, at] * un + as_[:, at] * us) + (aw[:, at] * uw + ae[:, at] * ue)
                 - dd[:, at] * u)
        return u + float(SUB) * drive

    guess_load.wait()

    @pl.when(j == 0)
    def _():
        init_load.wait()

    def first_window(w):
        at = window_at(w)
        wa[8:8 + tall, :] = st[:, at]
        fine(at)
        rs[:, cols(w, PAD, WINDOW)] = (wa[pl.ds(own + 8, rows), 128:128 + WINDOW]
                                       - gv[:, cols(w, 0, WINDOW)])

        @pl.when(even)
        def _():
            @pl.loop(0, per_window)
            def _(i):
                r_copy(w * per_window + i).start()

    @pl.loop(0, grains + 2)
    def _(i):
        @pl.when(jnp.logical_and(i < grains, j > 0))
        def _():
            guess_copy(i).wait_recv()
            forward(st, gh_send, gh_recv, i, GRAIN).start()

        g = i - 1

        @pl.when(jnp.logical_and(g >= 0, g < grains))
        def _():
            landed(st, gh_send, gh_recv, g, GRAIN).wait_recv()

        ratio = WINDOW // GRAIN

        @pl.when(jnp.logical_and(lax.rem(g + ratio, ratio) == 0, g > 0))
        def _():
            first_window(g // ratio - 1)

    def finish(c):
        at = cols(c, PAD)
        lo = pl.multiple_of(PAD + c * CHUNK, 128)
        tmp[...] = coarse(ee, lo)
        err = tmp[ownr, :] + rs[:, at]
        cor_ref[:, cols(c, 0)] = gv[:, cols(c, 0)] + err
        return err

    def second_window(w, fresh):
        at = window_at(w)
        wa[8:8 + tall, :] = st[:, at] + ee[:, at]
        if fresh:
            low = w * per_window + jnp.where(w == 0, 0, 1)
            high = jnp.minimum((w + 1) * per_window + 1, chunks)

            @pl.loop(low, high)
            def _(c):
                h_copy(c).wait_recv()

            wa[pl.ds(hal + 8, HALO), :] = st[halr, at] + eh[:, at]
        fine(at)
        out = cols(w, 0, WINDOW)
        res_ref[:, out] = wa[pl.ds(own + 8, rows), 128:128 + WINDOW] - cor_ref[:, out]

    @pl.when(odd)
    def _():
        @pl.loop(0, chunks + 2)
        def _(i):
            @pl.when(i < chunks)
            def _():
                r_copy(i).wait_recv()
                forward(rr, rh_send, rh_recv, i).start()

            c = i - 1

            @pl.when(jnp.logical_and(c >= 0, c < chunks))
            def _():
                @pl.when(takes_x)
                def _():
                    x_copy(c).wait_recv()
                    e_copy(c).start()
                    xh_copy(c, hal).wait_recv()

                landed(rr, rh_send, rh_recv, c).wait_recv()

            @pl.when(c >= 0)
            def _():
                lo = pl.multiple_of(PAD - 128 + c * CHUNK, 128)
                at = pl.ds(lo, CHUNK)
                ee[:, at] = coarse(ex, lo) + rr[:, at]

            @pl.when(c > 0)
            def _():
                er[:, cols(c - 1, 0)] = finish(c - 1)

                @pl.when(sends_x)
                def _():
                    x_copy(c - 1).start()
                    xh_copy(c - 1, there).start()

                h_copy(c - 1).start()

            late = per_window + 2
            ready = jnp.logical_and(c >= late, lax.rem(c + 2 * per_window - late, per_window) == 0)
            ready = jnp.logical_and(ready, c < late + (windows - 2) * per_window)

            @pl.when(jnp.logical_and(ready, jnp.logical_not(sends_x)))
            def _():
                second_window((c - late) // per_window, True)

        @pl.loop(jnp.where(sends_x, 0, windows - 2), windows)
        def _(w):
            second_window(w, True)

    @pl.when(even)
    def _():
        @pl.loop(0, chunks + 2)
        def _(i):
            @pl.when(jnp.logical_and(i < chunks, takes_e))
            def _():
                e_copy(i).wait_recv()
                forward(ee, eh_send, eh_recv, i).start()

            c = i - 1

            @pl.when(jnp.logical_and(jnp.logical_and(c >= 0, c < chunks), takes_e))
            def _():
                landed(ee, eh_send, eh_recv, c).wait_recv()

            @pl.when(c > 0)
            def _():
                finish(c - 1)

            @pl.when(jnp.logical_and(c > 0, lax.rem(c + per_window, per_window) == 0))
            def _():
                second_window(c // per_window - 1, False)

    for at in range(4):
        sib_copy(at, True).wait_send()

    @pl.loop(0, grains)
    def _(g):
        forward(st, gh_send, gh_recv, g, GRAIN).wait_send()

        @pl.when(has_next)
        def _():
            guess_copy(g).wait_send()

    @pl.loop(0, chunks)
    def _(c):
        @pl.when(even)
        def _():
            r_copy(c).wait_send()

        @pl.when(odd)
        def _():
            forward(rr, rh_send, rh_recv, c).wait_send()
            h_copy(c).wait_send()

        @pl.when(takes_x)
        def _():
            e_copy(c).wait_send()

        @pl.when(sends_x)
        def _():
            x_copy(c).wait_send()
            xh_copy(c, there).wait_send()

        @pl.when(takes_e)
        def _():
            forward(ee, eh_send, eh_recv, c).wait_send()


def local(initial, guess, source, kappa, speed_x, speed_y):
    count = lax.axis_size("tm")
    rows, n = kappa.shape
    chunks = n // CHUNK
    tall = rows + HALO
    wide_n = n + 2 * PAD
    sems = pltpu.SemaphoreType.DMA

    def vmem(*shape):
        return pltpu.VMEM(shape, jnp.float32)

    cor, res = pl.pallas_call(
        functools.partial(kernel, count),
        out_shape=[jax.ShapeDtypeStruct((rows, n), jnp.float32)] * 2,
        in_specs=[pl.BlockSpec(memory_space=pltpu.HBM)] * 6,
        out_specs=[pl.BlockSpec(memory_space=pltpu.VMEM)] * 2,
        scratch_shapes=[vmem(tall, wide_n)] * 14 + [
            vmem(rows, wide_n), vmem(HALO, wide_n), vmem(rows, n), vmem(rows, n),
            vmem(tall + 16, WINDOW + 256), vmem(tall + 16, WINDOW + 256), vmem(tall, CHUNK),
        ] + [sems((4,))] * 2 + [sems((6,))] + [sems((n // GRAIN,))] * 4 + [sems((chunks,))] * 14,
        compiler_params=pltpu.CompilerParams(
            collective_id=0, has_side_effects=True, vmem_limit_bytes=62 * 1024 * 1024
        ),
    )(initial, guess[0], source[0], kappa, speed_x, speed_y)
    return cor[None], res[None]


def solution(mesh):
    in_specs = (
        P(("groups", "space"), None),
        P(("groups", "tm"), "space", None),
        P(("groups", "tm"), "space", None),
        P("space", None),
        P("space", None),
        P("space", None),
    )
    out_specs = (P(("groups", "tm"), "space", None), P(("groups", "tm"), "space", None))
    return jax.shard_map(local, mesh=mesh, in_specs=in_specs, out_specs=out_specs, check_vma=False)
```
